256 devices in a mesh: dp: 8 (over y_hi, x), shard: 32 (over z, y_lo, core).
Axes of the slice: x: 4, y: 4 (y_hi: 2, y_lo: 2; y = y_hi * 2 + y_lo), z: 8, core: 2. Of those that a mesh axis runs over, the one named last changes fastest.
Arguments:
- tokens: bfloat16 [65536, 8192], P(('dp', 'shard')), may hold values from -6 to 6
- out_grad: bfloat16 [65536, 8192], P(('dp', 'shard')), may hold values from -0.0234375 to 0.0234375
- projector: bfloat16 [8192, 512], P(('dp', 'shard')), may hold values from -0.0625 to 0.0625
- first_moment: float32 [512, 8192], P('dp', 'shard'), may hold values from -6 to 6
- second_moment: float32 [512, 8192], P('dp', 'shard'), may hold values from 0.25 to 4
Outputs:
- first_new: float32 [512, 8192], P('dp', 'shard')
- second_new: float32 [512, 8192], P('dp', 'shard')
- update: bfloat16 [8192, 8192], P('dp', 'shard')
The draws below stay inside these ranges and needn't reach their ends.
All inputs are finite; a program needn't handle non-finite values.
Results may differ from the reference program's by a relative error of at most 0.0038.
The reference program's roundings to bfloat16 on the way (of `projected` and `direction`) count: a program that leaves them out, or rounds other values in their place, can miss the bound.
Values may be sent and summed in bfloat16 or wider, within the bound.
A program may use at most 128 MiB of HBM per device.

```python
import math
import jax
import jax.numpy as jnp
from jax import lax

D = 8192
RANK = 512
TOK_DEV = 256
TOKENS = 65536
N_DP = 8


def steps_of(rng, shape, split, low, high):
    level = 1.0
    for position, parts in split:
        heights = jax.random.uniform(jax.random.fold_in(jax.random.fold_in(rng, 6), position), (parts,), jnp.float32, low / len(split), high / len(split))
        level = level * jnp.repeat(jnp.exp(heights), shape[position] // parts).reshape((-1,) + (1,) * (len(shape) - 1 - position))
    return level


def gaussian(stream_key, shape, width, reach, cuts=(), kind=jnp.bfloat16):
    array = jax.random.normal(stream_key, shape, jnp.float32) * width
    if len(cuts) > 0:
        array = steps_of(stream_key, shape, cuts, -0.22, 0.18) * array
    return jnp.clip(array, min=-reach, max=reach).astype(kind)


def setup_inputs(seed: int = 0) -> dict:
    streams_of = jax.random.split(jax.random.key(seed), 6)
    return {
        "tokens": gaussian(streams_of[0], (TOKENS, D), 1.0, 6.0, ((0, 256),)),
        "out_grad": gaussian(streams_of[1], (TOKENS, D), (TOKENS ** -0.5), 0.0234375, ((0, 256),)),
        "projector": gaussian(streams_of[2], (D, RANK), D ** -0.5, 0.0625, ((0, 256),)),
        "first_moment": gaussian(streams_of[3], (RANK, D), 1.0, 6.0, ((0, 8), (1, 32)), jnp.float32),
        "second_moment": jnp.clip(jnp.exp(math.log(4.0) - 2.7725887 * jax.random.uniform(streams_of[4], (RANK, D), jnp.float32) ** steps_of(streams_of[4], (RANK, D), ((0, 8), (1, 32)), -0.2, 0.2)), 0.25, 4.0),
    }


beta_one = 0.9
beta_two = 0.999
adam_epsilon = 1e-08

def reference(tokens, out_grad, projector, first_moment, second_moment):
    block_rows = TOK_DEV * N_DP
    block_count = TOKENS // block_rows
    tok_blocks = tokens.reshape(block_count, block_rows, D)
    grad_blocks = out_grad.reshape(block_count, block_rows, D)

    def accumulate(running, inputs):
        tok_block, grad_block = inputs
        projected = jnp.dot(tok_block, projector, preferred_element_type=jnp.float32).astype(jnp.bfloat16)
        return (running + jnp.dot(projected.T, grad_block, preferred_element_type=jnp.float32), None)
    low_grad, _ = lax.scan(accumulate, jnp.zeros((RANK, D), jnp.float32), (tok_blocks, grad_blocks))
    first_new = beta_one * first_moment + (1.0 - beta_one) * low_grad
    second_new = beta_two * second_moment + (1.0 - beta_two) * low_grad * low_grad
    direction = (first_new / (jnp.sqrt(second_new) + adam_epsilon)).astype(jnp.bfloat16)
    update = jnp.dot(projector, direction, preferred_element_type=jnp.float32).astype(jnp.bfloat16)
    return (first_new, second_new, update)
```

```python
import jax
import jax.numpy as jnp
from jax import lax
from jax.experimental import pallas as pl
from jax.experimental.pallas import tpu as pltpu
from jax.sharding import PartitionSpec as P

MESH = pl.DeviceIdType.MESH
beta_one = 0.9
beta_two = 0.999
adam_epsilon = 1e-08
NX, NY, NZ = 4, 4, 8
NCH = 4
ZC = NZ // NCH
CW = ZC * 128
BF = jnp.bfloat16
F32 = jnp.float32


def kernel(tok_ref, grad_ref, proj_ref, m1_ref, m2_ref, o1_ref, o2_ref, up_ref,
           T, OG, S, W, LR, ACC, PJT, PT, RB1, RC1, SB, SC, RB2, RC2, T3, R3, D,
           loc_sem, ex_s, ex_r, zs, zr, ms, mr, fs, fr, lr_sem, pj_sem,
           s1, r1, s2, r2, s3, r3, ds, dr):
    dp = lax.axis_index("dp")
    sh = lax.axis_index("shard")
    x, yh = lax.rem(dp, NX), dp // NX
    z, yl, c = sh // 4, lax.rem(sh // 2, 2), lax.rem(sh, 2)
    y = yh * 2 + yl

    def dev(x_, y_, z_, c_):
        return ((y_ // 2) * NX + x_, z_ * 4 + lax.rem(y_, 2) * 2 + c_)

    def xp(k):
        return lax.rem(x + k, NX)

    def yp(k):
        return lax.rem(y + k, NY)

    def zp(k):
        return lax.rem(z + k, NZ)

    sib = dev(x, y, z, 1 - c)

    def rcopy(src, dst, ss, rs, device):
        return pltpu.make_async_remote_copy(src_ref=src, dst_ref=dst, send_sem=ss, recv_sem=rs,
                                            device_id=device, device_id_type=MESH)

    tok_own = pltpu.make_async_copy(tok_ref, T.at[c], loc_sem.at[0])
    tok_own.start()

    def og_src(par, cls, yl_, z_):
        return grad_ref.at[:, pl.ds(pl.multiple_of(z_ * 1024 + yl_ * 512 + par * 256 + cls * 128, 128), 128)]

    def og_dst(cls, yl_, z_):
        return OG.at[c, cls, yl_, z_ // ZC, :, pl.ds((z_ % ZC) * 128, 128)]

    for cls in range(2):
        for yl_ in range(2):
            for z_ in range(NZ):
                pltpu.make_async_copy(og_src(c, cls, yl_, z_), og_dst(cls, yl_, z_), loc_sem.at[1]).start()
    for h in range(2):
        for cls in range(2):
            S[h, cls] = proj_ref[:, h * 256 + cls * 128:h * 256 + cls * 128 + 128]

    barrier = pltpu.get_barrier_semaphore()
    peers = [sib]
    for k in range(1, NZ):
        peers += [dev(x, y, zp(k), c), dev(x, y, zp(k), 1 - c)]
    for k in range(1, 4):
        peers += [dev(xp(k), y, z, c), dev(x, yp(k), z, c), dev(xp(k), yp(2), z, c)]
    for p in peers:
        pl.semaphore_signal(barrier, inc=1, device_id=p, device_id_type=MESH)
    pl.semaphore_wait(barrier, len(peers))

    W[:, yh, x, z, yl, pl.ds(pl.multiple_of(c * 32, 32), 32), :] = S[c]
    z_copies = []
    for k in range(NZ):
        for rel in range(2):
            if k == 0 and rel == 0:
                continue
            t = c if rel == 0 else 1 - c
            cp = rcopy(S.at[t], W.at[:, yh, x, z, yl, pl.ds(pl.multiple_of(c * 32, 32), 32)],
                       zs.at[k, rel], zr.at[k, rel], dev(x, y, zp(k), t))
            cp.start()
            z_copies.append(cp)

    tok_ex = rcopy(tok_ref, T.at[c], ex_s.at[0], ex_r.at[0], sib)
    tok_ex.start()
    for cls in range(2):
        for yl_ in range(2):
            for z_ in range(NZ):
                rcopy(og_src(1 - c, cls, yl_, z_), og_dst(cls, yl_, z_), ex_s.at[1], ex_r.at[1], sib).start()
    og_ex = rcopy(OG.at[c], OG.at[1 - c], ex_s.at[1], ex_r.at[1], sib)

    for cp in z_copies:
        cp.wait()

    mid = [[None] * 4, [None] * 4]
    fin = []

    def forward(cls, j):
        if cls == 0:
            blk = W.at[0, yh, lax.rem(x + NX - j, NX), :, yl]
        else:
            q = lax.rem(y + NY - j, NY)
            blk = W.at[1, q // 2, x, :, lax.rem(q, 2)]
        for k in range(1, 4):
            to = dev(x, yp(k), z, c) if cls == 0 else dev(xp(k), y, z, c)
            cp = rcopy(blk, blk, fs.at[cls, j, k], fr.at[cls, j, k], to)
            cp.start()
            fin.append(cp)

    for k in range(1, 4):
        for cls in range(2):
            blk = W.at[cls, yh, x, :, yl]
            to = dev(xp(k), y, z, c) if cls == 0 else dev(x, yp(k), z, c)
            mid[cls][k] = rcopy(blk, blk, ms.at[cls, k], mr.at[cls, k], to)
            mid[cls][k].start()
    for cls in range(2):
        forward(cls, 0)
    for j in (1, 3, 2):
        for cls in range(2):
            mid[cls][j].wait_recv()
            forward(cls, j)
    for j in range(1, 4):
        for cls in range(2):
            mid[cls][j].wait_send()
    for cp in fin:
        cp.wait()

    lr_copy = rcopy(W.at[:, yh, x], LR, lr_sem.at[0], lr_sem.at[1], sib)
    lr_copy.start()
    tok_own.wait()
    tok_ex.wait()

    ACC[...] = jnp.zeros_like(ACC)

    def proj_step(k, _):
        w0 = W[0, k // 4, lax.rem(k, 4)].reshape(1024, 128)
        w1 = W[1, k // 4, lax.rem(k, 4)].reshape(1024, 128)
        w = jnp.concatenate([w0, w1], axis=1)
        for t in range(2):
            tk = T[t, :, pl.ds(pl.multiple_of(k * 1024, 1024), 1024)]
            ACC[pl.ds(t * 256, 256), :] += jnp.dot(tk, w, preferred_element_type=F32)
        return 0

    lax.fori_loop(0, 8, proj_step, 0)
    PJT[c] = ACC[...].T.astype(BF)
    pj_copy = rcopy(PJT.at[c], PJT.at[c], pj_sem.at[0], pj_sem.at[1], sib)
    pj_copy.start()
    pltpu.make_async_copy(OG.at[c], OG.at[c], loc_sem.at[1]).wait()
    og_ex.wait()
    pj_copy.wait()

    ph1, ph2 = [], []
    for ch in range(NCH):
        def part_step(i, _, ch=ch):
            cls, yl_ = i // 2, lax.rem(i, 2)
            for r in range(2):
                v = jnp.dot(PJT[r, :, 0:256], OG[0, cls, yl_, ch], preferred_element_type=F32)
                v = v + jnp.dot(PJT[r, :, 256:512], OG[1, cls, yl_, ch], preferred_element_type=F32)
                PT[cls, ch, yl_, r] = v.astype(BF).reshape(4, 64, CW)
            return 0

        lax.fori_loop(0, 4, part_step, 0)
        cps = []
        for k in range(1, 4):
            q = yp(k)
            cps.append(rcopy(PT.at[0, ch, lax.rem(q, 2), q // 2], RB1.at[ch, k - 1],
                             s1.at[0, ch, k], r1.at[0, ch, k], dev(x, q, z, c)))
            cps.append(rcopy(PT.at[1, ch, :, :, xp(k)], RC1.at[ch, k - 1],
                             s1.at[1, ch, k], r1.at[1, ch, k], dev(xp(k), y, z, c)))
        for cp in cps:
            cp.start()
        ph1.append(cps)

    ph3 = []
    for step in range(NCH + 1):
        if step < NCH:
            ch = step
            for cp in ph1[ch]:
                cp.wait_recv()
            vb = PT[0, ch, yl, yh].astype(F32)
            vc = PT[1, ch, :, :, x].astype(F32)
            for k in range(3):
                vb = vb + RB1[ch, k].astype(F32)
                vc = vc + RC1[ch, k].astype(F32)
            SB[ch] = vb
            SC[ch] = vc
            cps = []
            for k in range(1, 4):
                q = yp(k)
                cps.append(rcopy(SB.at[ch, xp(k)], RB2.at[ch, k - 1],
                                 s2.at[0, ch, k], r2.at[0, ch, k], dev(xp(k), y, z, c)))
                cps.append(rcopy(SC.at[ch, lax.rem(q, 2), q // 2], RC2.at[ch, k - 1],
                                 s2.at[1, ch, k], r2.at[1, ch, k], dev(x, q, z, c)))
            for cp in cps:
                cp.start()
            ph2.append(cps)
        if step >= 1:
            ch = step - 1
            for cp in ph2[ch]:
                cp.wait_recv()
            vb = SB[ch, x] + RB2[ch, 0] + RB2[ch, 1] + RB2[ch, 2]
            vc = SC[ch, yl, yh] + RC2[ch, 0] + RC2[ch, 1] + RC2[ch, 2]
            for i in range(ZC):
                T3[ch * ZC + i, 0] = vb[:, i * 128:(i + 1) * 128]
                T3[ch * ZC + i, 1] = vc[:, i * 128:(i + 1) * 128]
                to = ch * ZC + i

                @pl.when(to != z)
                def _(to=to):
                    rcopy(T3.at[to], R3.at[z], s3.at[to], r3.at[z], dev(x, y, to, c)).start()

    R3[z] = T3[z]
    for k in range(1, NZ):
        q = zp(k)
        rcopy(T3.at[q], R3.at[q], s3.at[q], r3.at[q], dev(x, y, q, c)).wait()

    g0 = R3[0]
    for k in range(1, NZ):
        g0 = g0 + R3[k]
    g = jnp.concatenate([g0[0], g0[1]], axis=1)
    first = beta_one * m1_ref[...] + (1.0 - beta_one) * g
    second = beta_two * m2_ref[...] + (1.0 - beta_two) * g * g
    o1_ref[...] = first
    o2_ref[...] = second
    D[dp] = (first / (jnp.sqrt(second) + adam_epsilon)).astype(BF)
    d_copies = []
    for k in range(1, 8):
        q = lax.rem(dp + k, 8)
        cp = rcopy(D.at[dp], D.at[dp], ds.at[k], dr.at[k], (q, sh))
        cp.start()
        d_copies.append(cp)
    for cps in ph1 + ph2:
        for cp in cps:
            cp.wait_send()
    lr_copy.wait()
    for cp in d_copies:
        cp.wait()
    d_own = D[pl.ds(c * 4, 4)].reshape(256, 256)
    d_sib = D[pl.ds((1 - c) * 4, 4)].reshape(256, 256)
    for b in range(4):
        own = jnp.concatenate([W[h, yh, x, 2 * b:2 * b + 2].reshape(256, 128) for h in range(2)], axis=1)
        oth = jnp.concatenate([LR[h, 2 * b:2 * b + 2].reshape(256, 128) for h in range(2)], axis=1)
        u = jnp.dot(own, d_own, preferred_element_type=F32) + jnp.dot(oth, d_sib, preferred_element_type=F32)
        up_ref[b * 256:(b + 1) * 256, :] = u.astype(BF)


def on_device(tokens, out_grad, projector, first_moment, second_moment):
    vm = pl.BlockSpec(memory_space=pltpu.VMEM)
    hbm = pl.BlockSpec(memory_space=pl.ANY)
    dma = pltpu.SemaphoreType.DMA
    return pl.pallas_call(
        kernel,
        out_shape=(
            jax.ShapeDtypeStruct((64, 256), F32),
            jax.ShapeDtypeStruct((64, 256), F32),
            jax.ShapeDtypeStruct((1024, 256), BF),
        ),
        in_specs=[hbm, hbm, vm, vm, vm],
        out_specs=(vm, vm, vm),
        scratch_shapes=[
            pltpu.VMEM((2, 256, 8192), BF),
            pltpu.VMEM((2, 2, 2, NCH, 256, CW), BF),
            pltpu.VMEM((2, 2, 32, 128), BF),
            pltpu.VMEM((2, 2, 4, 8, 2, 64, 128), BF),
            pltpu.VMEM((2, 8, 2, 64, 128), BF),
            pltpu.VMEM((512, 256), F32),
            pltpu.VMEM((2, 256, 512), BF),
            pltpu.VMEM((2, NCH, 2, 2, 4, 64, CW), BF),
            pltpu.VMEM((NCH, 3, 4, 64, CW), BF),
            pltpu.VMEM((NCH, 3, 2, 2, 64, CW), BF),
            pltpu.VMEM((NCH, 4, 64, CW), F32),
            pltpu.VMEM((NCH, 2, 2, 64, CW), F32),
            pltpu.VMEM((NCH, 3, 64, CW), F32),
            pltpu.VMEM((NCH, 3, 64, CW), F32),
            pltpu.VMEM((8, 2, 64, 128), F32),
            pltpu.VMEM((8, 2, 64, 128), F32),
            pltpu.VMEM((8, 64, 256), BF),
            dma((2,)), dma((2,)), dma((2,)),
            dma((8, 2)), dma((8, 2)),
            dma((2, 4)), dma((2, 4)),
            dma((2, 4, 4)), dma((2, 4, 4)),
            dma((2,)), dma((2,)),
            dma((2, NCH, 4)), dma((2, NCH, 4)),
            dma((2, NCH, 4)), dma((2, NCH, 4)),
            dma((8,)), dma((8,)),
            dma((8,)), dma((8,)),
        ],
        compiler_params=pltpu.CompilerParams(
            collective_id=0, has_side_effects=True, vmem_limit_bytes=56 * 2**20
        ),
        name="galore",
    )(tokens, out_grad, projector, first_moment, second_moment)


def solution(mesh):
    in_specs = (
        P(("dp", "shard"), None),
        P(("dp", "shard"), None),
        P(("dp", "shard"), None),
        P("dp", "shard"),
        P("dp", "shard"),
    )
    out_specs = (P("dp", "shard"), P("dp", "shard"), P("dp", "shard"))
    return jax.shard_map(
        on_device, mesh=mesh, in_specs=in_specs, out_specs=out_specs, check_vma=False
    )
```

```python
import jax
import jax.numpy as jnp
from jax import lax
from jax.experimental import pallas as pl
from jax.experimental.pallas import tpu as pltpu
from jax.sharding import PartitionSpec as P

MESH = pl.DeviceIdType.MESH
beta_one = 0.9
beta_two = 0.999
adam_epsilon = 1e-08
NX, NY, NZ = 4, 4, 8
NCH = 4
ZC = NZ // NCH
CW = ZC * 128
BF = jnp.bfloat16
F32 = jnp.float32


def kernel(tok_ref, grad_ref, proj_ref, m1_ref, m2_ref, o1_ref, o2_ref, up_ref,
           T, OG, PJ, M1, M2, S, W, LR, ACC, PJT, PT, PF, RL, AGB, R1, SB, SC, R2, T3, R3, D,
           loc_sem, ex_s, ex_r, zr, mr, fr, lr_sem, pj_sem, r1, rf, r2, snd, rcv):
    dp = lax.axis_index("dp")
    sh = lax.axis_index("shard")
    x, yh = lax.rem(dp, NX), dp // NX
    z, yl, c = sh // 4, lax.rem(sh // 2, 2), lax.rem(sh, 2)
    y = yh * 2 + yl

    def dev(x_, y_, z_, c_):
        return ((y_ // 2) * NX + x_, z_ * 4 + lax.rem(y_, 2) * 2 + c_)

    def xp(k):
        return lax.rem(x + k, NX)

    def yp(k):
        return lax.rem(y + k, NY)

    def zp(k):
        return lax.rem(z + k, NZ)

    sib = dev(x, y, z, 1 - c)

    def arrived(rows, columns, sem):
        ref = T.at[0, 0:rows, 0:columns]
        pltpu.make_async_copy(ref, ref, sem).wait()

    def rcopy(src, dst, ss, rs, device):
        return pltpu.make_async_remote_copy(src_ref=src, dst_ref=dst, send_sem=ss, recv_sem=rs,
                                            device_id=device, device_id_type=MESH)

    barrier = pltpu.get_barrier_semaphore()
    peers = [sib]
    for k in range(1, NZ):
        peers += [dev(x, y, zp(k), c), dev(x, y, zp(k), 1 - c)]
    for k in range(1, 4):
        peers += [dev(xp(k), y, z, c), dev(x, yp(k), z, c), dev(xp(k), yp(2), z, c)]
    for p in peers:
        pl.semaphore_signal(barrier, inc=1, device_id=p, device_id_type=MESH)

    tok_own = pltpu.make_async_copy(tok_ref, T.at[c], loc_sem.at[0])
    pj_own = pltpu.make_async_copy(proj_ref, PJ, loc_sem.at[2])
    pj_own.start()
    m_own = [pltpu.make_async_copy(m1_ref, M1, loc_sem.at[3]), pltpu.make_async_copy(m2_ref, M2, loc_sem.at[4])]
    for cp in m_own:
        cp.start()
    tok_own.start()

    def og_src(par, cls, yl_, z_):
        return grad_ref.at[:, pl.ds(pl.multiple_of(z_ * 1024 + yl_ * 512 + par * 256 + cls * 128, 128), 128)]

    def og_dst(cls, yl_, z_):
        return OG.at[c, cls, yl_, z_ // ZC, :, pl.ds((z_ % ZC) * 128, 128)]

    for cls in range(2):
        for yl_ in range(2):
            for z_ in range(NZ):
                pltpu.make_async_copy(og_src(c, cls, yl_, z_), og_dst(cls, yl_, z_), loc_sem.at[1]).start()

    pj_own.wait()
    for h in range(2):
        for cls in range(2):
            S[h, cls] = PJ[:, h * 256 + cls * 128:h * 256 + cls * 128 + 128]
    pl.semaphore_wait(barrier, len(peers))

    W[:, yh, x, z, yl, pl.ds(pl.multiple_of(c * 32, 32), 32), :] = S[c]
    z_order = (0, 1, 7, 2, 6, 3, 5, 4)
    for k in z_order:
        for rel in range(2):
            if k == 0 and rel == 0:
                continue
            t = c if rel == 0 else 1 - c
            cp = rcopy(S.at[t], W.at[:, yh, x, z, yl, pl.ds(pl.multiple_of(c * 32, 32), 32)],
                       snd.at[0], zr.at[k], dev(x, y, zp(k), t))
            cp.start()


    def proj_step(k):
        w0 = W[0, k // 4, lax.rem(k, 4)].reshape(1024, 128)
        w1 = W[1, k // 4, lax.rem(k, 4)].reshape(1024, 128)
        w = jnp.concatenate([w0, w1], axis=1)
        tk = T[:, :, pl.ds(pl.multiple_of(k * 1024, 1024), 1024)].reshape(512, 1024)
        ACC[...] += jnp.dot(tk, w, preferred_element_type=F32)
        return 0


    def line(cls, k):
        return dev(x, yp(k), z, c) if cls == 0 else dev(xp(k), y, z, c)

    def block(cls, j, k, zs_):
        xb = lax.rem(x + NX - (j if cls == 0 else k), NX)
        yb = lax.rem(y + NY - (k if cls == 0 else j), NY)
        return W.at[cls, yb // 2, xb, zs_, lax.rem(yb, 2)]

    whole_z, low_z, high_z = pl.ds(0, NZ), pl.ds(0, NZ // 2), pl.ds(NZ // 2, NZ // 2)

    def send(cls, j, key, blk, k):
        rcopy(blk, blk, snd.at[1], fr.at[cls, j, key], line(cls, k)).start()

    def forward(cls, j):
        for k in (1, 3):
            send(cls, j, k // 2, block(cls, j, 0, whole_z), k)

    def relay(cls, j):
        arrived(16, 4096, fr.at[cls, j, 0])
        send(cls, j, 2, block(cls, j, 1, low_z), 1)
        arrived(16, 4096, fr.at[cls, j, 1])
        send(cls, j, 2, block(cls, j, 3, high_z), 3)

    for k in z_order:
        arrived(16, 512 if k == 0 else 1024, zr.at[k])
        for cls in range(2):
            blk = W.at[cls, yh, x, lax.rem(z + NZ - k, NZ), yl]
            for m in (1, 3, 2):
                to = dev(xp(m), y, z, c) if cls == 0 else dev(x, yp(m), z, c)
                rcopy(blk, blk, snd.at[2], mr.at[cls, m], to).start()
            for m in (1, 3):
                send(cls, 0, m // 2, blk, m)

    tok_ex = rcopy(tok_ref, T.at[c], ex_s.at[0], ex_r.at[0], sib)
    tok_ex.start()
    for cls in range(2):
        for yl_ in range(2):
            for z_ in range(NZ):
                rcopy(og_src(1 - c, cls, yl_, z_), og_dst(cls, yl_, z_), ex_s.at[1], ex_r.at[1], sib).start()
    og_ex = rcopy(OG.at[c], OG.at[1 - c], ex_s.at[1], ex_r.at[1], sib)

    for j in (1, 3, 2):
        for cls in range(2):
            arrived(16, 4096, mr.at[cls, j])
            forward(cls, j)
        for cls in range(2):
            relay(cls, 0 if j == 1 else 1 if j == 3 else 3)
    for cls in range(2):
        relay(cls, 2)
    tok_own.wait()
    tok_ex.wait()
    ACC[...] = jnp.zeros_like(ACC)
    for j in (0, 1, 3):
        for cls in range(2):
            arrived(16, 4096, fr.at[cls, j, 2])
    lax.fori_loop(0, 3, lambda i, _: proj_step(yh * 4 + lax.rem(x + 3 + i, NX)), 0)
    for cls in range(2):
        arrived(16, 4096, fr.at[cls, 2, 2])

    lr_copy = rcopy(W.at[:, yh, x], LR, lr_sem.at[0], lr_sem.at[1], sib)
    lr_copy.start()
    proj_step(yh * 4 + lax.rem(x + 2, NX))
    lax.fori_loop(0, 4, lambda i, _: proj_step((1 - yh) * 4 + i), 0)
    PJT[c] = ACC[...].T.astype(BF)
    pj_copy = rcopy(PJT.at[c], PJT.at[c], pj_sem.at[0], pj_sem.at[1], sib)
    pj_copy.start()
    pltpu.make_async_copy(OG.at[c], OG.at[c], loc_sem.at[1]).wait()
    og_ex.wait()

    def chunk(j):
        return lax.rem(z // ZC + 1 + j, NCH)

    def part(j, r):
        def part_step(i, _):
            cls, yl_ = i // 2, lax.rem(i, 2)
            v = jnp.dot(PJT[r, :, 0:256], OG[0, cls, yl_, chunk(j)], preferred_element_type=F32)
            v = v + jnp.dot(PJT[r, :, 256:512], OG[1, cls, yl_, chunk(j)], preferred_element_type=F32)
            PF[cls, j, yl_, r] = v.reshape(4, 64, CW)
            PT[cls, j, yl_, r] = v.astype(BF).reshape(4, 64, CW)
            return 0

        lax.fori_loop(0, 4, part_step, 0, unroll=True)

    KD = (1, 3)

    def half(ref, cls, j, k, h):
        if cls == 0:
            q = yp(k)
            return ref.at[0, j, lax.rem(q, 2), q // 2, 2 * h:2 * h + 2]
        return ref.at[1, j, h, :, xp(k)]

    relays = {}

    def send_partials(j):
        for cls in range(2):
            for d in range(2):
                cp = rcopy(half(PT, cls, j, 2, d), RL.at[cls, j, d], snd.at[3], r1.at[cls, j, d], line(cls, KD[d]))
                cp.start()
                relays[cls, j, d] = cp
        for cls in range(2):
            for d in range(2):
                rcopy(half(PT, cls, j, KD[d], 1 - d), R1.at[j, cls, d, 1 - d], snd.at[3], rf.at[j],
                      line(cls, KD[d])).start()

    def relay_partials(j):
        for d in range(2):
            for cls in range(2):
                relays[cls, j, d].wait_recv()
                AGB[cls, j, d] = (half(PF, cls, j, KD[d], d)[...] + RL[cls, j, d].astype(F32)).astype(BF)
                rcopy(AGB.at[cls, j, d], R1.at[j, cls, d, d], snd.at[4], rf.at[j], line(cls, KD[d])).start()

    def first_sums(j):
        arrived(32, 8192, rf.at[j])
        for h in range(2):
            SB[j, 2 * h:2 * h + 2] = half(PF, 0, j, 0, h)[...] + R1[j, 0, 0, h].astype(F32) + R1[j, 0, 1, h].astype(F32)
            SC[j, h] = half(PF, 1, j, 0, h)[...] + R1[j, 1, 0, h].astype(F32) + R1[j, 1, 1, h].astype(F32)
        for k in (2, 1, 3):
            q = yp(k)
            rcopy(SB.at[j, xp(k)], R2.at[j, 0, k - 1], snd.at[5], r2.at[j], dev(xp(k), y, z, c)).start()
            rcopy(SC.at[j, lax.rem(q, 2), q // 2], R2.at[j, 1, k - 1], snd.at[5], r2.at[j], dev(x, q, z, c)).start()

    def second_sums(j):
        arrived(48, 4096, r2.at[j])
        vb = SB[j, x] + R2[j, 0, 0] + R2[j, 0, 1] + R2[j, 0, 2]
        vc = SC[j, yl, yh] + R2[j, 1, 0] + R2[j, 1, 1] + R2[j, 1, 2]
        for i in range(ZC):
            to = chunk(j) * ZC + i
            T3[to, 0] = vb[:, i * 128:(i + 1) * 128]
            T3[to, 1] = vc[:, i * 128:(i + 1) * 128]

            @pl.when(to != z)
            def _(to=to):
                rcopy(T3.at[to], R3.at[z], snd.at[6], rcv.at[2], dev(x, y, to, c)).start()

    for step in range(NCH + 3):
        if step < NCH:
            part(step, c)
            if step == 0:
                pj_copy.wait()
            part(step, 1 - c)
            send_partials(step)
        if 0 <= step - 1 < NCH:
            relay_partials(step - 1)
        if 0 <= step - 2 < NCH:
            first_sums(step - 2)
        if 0 <= step - 3 < NCH:
            second_sums(step - 3)

    R3[z] = T3[z]
    arrived(112, 2048, rcv.at[2])

    g0 = R3[0]
    for k in range(1, NZ):
        g0 = g0 + R3[k]
    g = jnp.concatenate([g0[0], g0[1]], axis=1)
    for cp in m_own:
        cp.wait()
    first = beta_one * M1[...] + (1.0 - beta_one) * g
    second = beta_two * M2[...] + (1.0 - beta_two) * g * g
    o1_ref[...] = first
    o2_ref[...] = second
    D[dp] = (first / (jnp.sqrt(second) + adam_epsilon)).astype(BF)
    for k in range(1, 8):
        q = lax.rem(dp + k, 8)
        rcopy(D.at[dp], D.at[dp], snd.at[7], rcv.at[3], (q, sh)).start()
    arrived(240, 512, snd.at[0])
    arrived(192, 8192, snd.at[1])
    arrived(48, 8192, snd.at[2])
    arrived(128, 8192, snd.at[3])
    arrived(64, 8192, snd.at[4])
    arrived(96, 8192, snd.at[5])
    arrived(112, 2048, snd.at[6])
    lr_copy.wait()
    arrived(112, 1024, rcv.at[3])
    arrived(112, 1024, snd.at[7])
    d_own = D[pl.ds(c * 4, 4)].reshape(256, 256)
    d_sib = D[pl.ds((1 - c) * 4, 4)].reshape(256, 256)
    for b in range(4):
        own = jnp.concatenate([W[h, yh, x, 2 * b:2 * b + 2].reshape(256, 128) for h in range(2)], axis=1)
        oth = jnp.concatenate([LR[h, 2 * b:2 * b + 2].reshape(256, 128) for h in range(2)], axis=1)
        u = jnp.dot(own, d_own, preferred_element_type=F32) + jnp.dot(oth, d_sib, preferred_element_type=F32)
        up_ref[b * 256:(b + 1) * 256, :] = u.astype(BF)


def store_outputs(a_ref, b_ref, u_ref, ao_ref, bo_ref, uo_ref, sem):
    copies = [
        pltpu.make_async_copy(u_ref, uo_ref, sem.at[0]),
        pltpu.make_async_copy(a_ref, ao_ref, sem.at[1]),
        pltpu.make_async_copy(b_ref, bo_ref, sem.at[2]),
    ]
    for cp in copies:
        cp.start()
    for cp in copies:
        cp.wait()


def on_device(tokens, out_grad, projector, first_moment, second_moment):
    vm = pl.BlockSpec(memory_space=pltpu.VMEM)
    hbm = pl.BlockSpec(memory_space=pl.ANY)
    dma = pltpu.SemaphoreType.DMA
    held = pl.pallas_call(
        kernel,
        out_shape=(pltpu.VMEM((64, 256), F32), pltpu.VMEM((64, 256), F32), pltpu.VMEM((1024, 256), BF)),
        in_specs=[pl.BlockSpec(memory_space=pltpu.HBM)] * 5,
        out_specs=(vm, vm, vm),
        scratch_shapes=[
            pltpu.VMEM((2, 256, 8192), BF),
            pltpu.VMEM((2, 2, 2, NCH, 256, CW), BF),
            pltpu.VMEM((32, 512), BF),
            pltpu.VMEM((64, 256), F32),
            pltpu.VMEM((64, 256), F32),
            pltpu.VMEM((2, 2, 32, 128), BF),
            pltpu.VMEM((2, 2, 4, 8, 2, 64, 128), BF),
            pltpu.VMEM((2, 8, 2, 64, 128), BF),
            pltpu.VMEM((512, 256), F32),
            pltpu.VMEM((2, 256, 512), BF),
            pltpu.VMEM((2, NCH, 2, 2, 4, 64, CW), BF),
            pltpu.VMEM((2, NCH, 2, 2, 4, 64, CW), F32),
            pltpu.VMEM((2, NCH, 2, 2, 64, CW), BF),
            pltpu.VMEM((2, NCH, 2, 2, 64, CW), BF),
            pltpu.VMEM((NCH, 2, 2, 2, 2, 64, CW), BF),
            pltpu.VMEM((NCH, 4, 64, CW), F32),
            pltpu.VMEM((NCH, 2, 2, 64, CW), F32),
            pltpu.VMEM((NCH, 2, 3, 64, CW), F32),
            pltpu.VMEM((8, 2, 64, 128), F32),
            pltpu.VMEM((8, 2, 64, 128), F32),
            pltpu.VMEM((8, 64, 256), BF),
            dma((5,)), dma((2,)), dma((2,)),
            dma((8,)), dma((2, 4)), dma((2, 4, 3)),
            dma((2,)), dma((2,)),
            dma((2, NCH, 2)), dma((NCH,)), dma((NCH,)),
            dma((8,)), dma((4,)),
        ],
        compiler_params=pltpu.CompilerParams(
            collective_id=0, has_side_effects=True, vmem_limit_bytes=56 * 2**20
        ),
        name="galore",
    )(tokens, out_grad, projector, first_moment, second_moment)
    return pl.pallas_call(
        store_outputs,
        out_shape=(
            jax.ShapeDtypeStruct((64, 256), F32),
            jax.ShapeDtypeStruct((64, 256), F32),
            jax.ShapeDtypeStruct((1024, 256), BF),
        ),
        in_specs=[vm, vm, vm],
        out_specs=(hbm, hbm, hbm),
        scratch_shapes=[dma((3,))],
        name="store_outputs",
    )(*[pltpu.with_memory_space_constraint(a, pltpu.VMEM) for a in held])


def solution(mesh):
    in_specs = (
        P(("dp", "shard"), None),
        P(("dp", "shard"), None),
        P(("dp", "shard"), None),
        P("dp", "shard"),
        P("dp", "shard"),
    )
    out_specs = (P("dp", "shard"), P("dp", "shard"), P("dp", "shard"))
    return jax.shard_map(
        on_device, mesh=mesh, in_specs=in_specs, out_specs=out_specs, check_vma=False
    )
```

```python
import jax
import jax.numpy as jnp
from jax import lax
from jax.experimental import pallas as pl
from jax.experimental.pallas import tpu as pltpu
from jax.sharding import PartitionSpec as P

MESH = pl.DeviceIdType.MESH
beta_one = 0.9
beta_two = 0.999
adam_epsilon = 1e-08
NX, NY, NZ = 4, 4, 8
NCH = 4
ZC = NZ // NCH
CW = ZC * 128
BF = jnp.bfloat16
F32 = jnp.float32


def kernel(tok_ref, grad_ref, proj_ref, m1_ref, m2_ref, o1_ref, o2_ref, up_ref,
           T, OG, OGX, PJX, PJ, M1, M2, S, W, LR, ACC, PJT, PT, PF, RL, AGB, R1, SB, SC, R2, T3, R3, D,
           loc_sem, ex_s, ex_r, zr, mr, fr, lr_sem, pj_sem, r1, rf, r2, snd, rcv):
    dp = lax.axis_index("dp")
    sh = lax.axis_index("shard")
    x, yh = lax.rem(dp, NX), dp // NX
    z, yl, c = sh // 4, lax.rem(sh // 2, 2), lax.rem(sh, 2)
    y = yh * 2 + yl

    def dev(x_, y_, z_, c_):
        return ((y_ // 2) * NX + x_, z_ * 4 + lax.rem(y_, 2) * 2 + c_)

    def xp(k):
        return lax.rem(x + k, NX)

    def yp(k):
        return lax.rem(y + k, NY)

    def zp(k):
        return lax.rem(z + k, NZ)

    sib = dev(x, y, z, 1 - c)
    p = lax.rem(z, 2)
    zq = z + 1 - 2 * p

    def chunk(j):
        return lax.rem(z // ZC + 1 + j, NCH)

    def arrived(rows, columns, sem):
        ref = T.at[0, 0:rows, 0:columns]
        pltpu.make_async_copy(ref, ref, sem).wait()

    def rcopy(src, dst, ss, rs, device):
        return pltpu.make_async_remote_copy(src_ref=src, dst_ref=dst, send_sem=ss, recv_sem=rs,
                                            device_id=device, device_id_type=MESH)

    barrier = pltpu.get_barrier_semaphore()
    peers = [sib]
    for k in range(1, NZ):
        peers += [dev(x, y, zp(k), c), dev(x, y, zp(k), 1 - c)]
    for k in range(1, 4):
        peers += [dev(xp(k), y, z, c), dev(x, yp(k), z, c), dev(xp(k), yp(2), z, c)]
    for peer in peers:
        pl.semaphore_signal(barrier, inc=1, device_id=peer, device_id_type=MESH)

    tok_own = pltpu.make_async_copy(tok_ref, T.at[c], loc_sem.at[0])
    pj_own = pltpu.make_async_copy(proj_ref, PJ, loc_sem.at[2])
    pj_own.start()
    m_own = [pltpu.make_async_copy(m1_ref, M1, loc_sem.at[3]), pltpu.make_async_copy(m2_ref, M2, loc_sem.at[4])]
    for cp in m_own:
        cp.start()
    tok_own.start()

    def og_src(par, cls, yl_, z_):
        return grad_ref.at[:, pl.ds(pl.multiple_of(z_ * 1024 + yl_ * 512 + par * 256 + cls * 128, 128), 128)]

    def og_dst(cls, yl_, z_):
        return OG.at[c, cls, yl_, z_ // ZC, :, pl.ds((z_ % ZC) * 128, 128)]

    for cls in range(2):
        for yl_ in range(2):
            for z_ in range(NZ):
                pltpu.make_async_copy(og_src(c, cls, yl_, z_), og_dst(cls, yl_, z_), loc_sem.at[1]).start()

    pj_own.wait()
    for h in range(2):
        for cls in range(2):
            S[h, cls] = PJ[:, h * 256 + cls * 128:h * 256 + cls * 128 + 128]
    pl.semaphore_wait(barrier, len(peers))

    W[:, yh, x, z, yl, pl.ds(pl.multiple_of(c * 32, 32), 32), :] = S[c]
    z_order = (0, 1, 7, 2, 6, 3, 5, 4)
    for k in z_order:
        for rel in range(2):
            if k == 0 and rel == 0:
                continue
            t = c if rel == 0 else 1 - c
            cp = rcopy(S.at[t], W.at[:, yh, x, z, yl, pl.ds(pl.multiple_of(c * 32, 32), 32)],
                       snd.at[0], zr.at[k], dev(x, y, zp(k), t))
            cp.start()


    def proj_step(k):
        w0 = W[0, k // 4, lax.rem(k, 4)].reshape(1024, 128)
        w1 = W[1, k // 4, lax.rem(k, 4)].reshape(1024, 128)
        w = jnp.concatenate([w0, w1], axis=1)
        tk = T[:, :, pl.ds(pl.multiple_of(k * 1024, 1024), 1024)].reshape(512, 1024)
        ACC[...] += jnp.dot(tk, w, preferred_element_type=F32)
        return 0


    def line(cls, k):
        return dev(x, yp(k), z, c) if cls == 0 else dev(xp(k), y, z, c)

    def block(cls, j, k, zs_):
        xb = lax.rem(x + NX - (j if cls == 0 else k), NX)
        yb = lax.rem(y + NY - (k if cls == 0 else j), NY)
        return W.at[cls, yb // 2, xb, zs_, lax.rem(yb, 2)]

    whole_z, low_z, high_z = pl.ds(0, NZ), pl.ds(0, NZ // 2), pl.ds(NZ // 2, NZ // 2)

    def send(cls, j, key, blk, k):
        rcopy(blk, blk, snd.at[1], fr.at[cls, j, key], line(cls, k)).start()

    def forward(cls, j):
        for k in (1, 3):
            send(cls, j, k // 2, block(cls, j, 0, whole_z), k)

    def relay(cls, j):
        arrived(16, 4096, fr.at[cls, j, 0])
        send(cls, j, 2, block(cls, j, 1, low_z), 1)
        arrived(16, 4096, fr.at[cls, j, 1])
        send(cls, j, 2, block(cls, j, 3, high_z), 3)

    for k in z_order:
        arrived(16, 512 if k == 0 else 1024, zr.at[k])
        for cls in range(2):
            blk = W.at[cls, yh, x, lax.rem(z + NZ - k, NZ), yl]
            for m in (1, 3, 2):
                to = dev(xp(m), y, z, c) if cls == 0 else dev(x, yp(m), z, c)
                rcopy(blk, blk, snd.at[2], mr.at[cls, m], to).start()
            for m in (1, 3):
                send(cls, 0, m // 2, blk, m)

    tok_ex = rcopy(tok_ref, T.at[c], ex_s.at[0], ex_r.at[0], sib)
    tok_ex.start()
    for cls in range(2):
        for yl_ in range(2):
            for z_ in range(NZ):
                rcopy(og_src(1 - c, cls, yl_, z_), og_dst(cls, yl_, z_), ex_s.at[1], ex_r.at[1], sib).start()
    og_ex = rcopy(OG.at[c], OG.at[1 - c], ex_s.at[1], ex_r.at[1], sib)
    for jj in range(2):
        for cls in range(2):
            for yl_ in range(2):
                for c_ in range(2):
                    rcopy(og_src(c_, cls, yl_, chunk(2 + jj) * ZC + 1 - p), OGX.at[c, cls, yl_, jj],
                          snd.at[8], rcv.at[0], dev(x, y, zq, c_)).start()

    for j in (1, 3, 2):
        for cls in range(2):
            arrived(16, 4096, mr.at[cls, j])
            forward(cls, j)
        for cls in range(2):
            relay(cls, 0 if j == 1 else 1 if j == 3 else 3)
    for cls in range(2):
        relay(cls, 2)
    tok_own.wait()
    tok_ex.wait()
    ACC[...] = jnp.zeros_like(ACC)
    for j in (0, 1, 3):
        for cls in range(2):
            arrived(16, 4096, fr.at[cls, j, 2])
    lax.fori_loop(0, 3, lambda i, _: proj_step(yh * 4 + lax.rem(x + 3 + i, NX)), 0)
    for cls in range(2):
        arrived(16, 4096, fr.at[cls, 2, 2])

    lr_copy = rcopy(W.at[:, yh, x], LR, lr_sem.at[0], lr_sem.at[1], sib)
    lr_copy.start()
    proj_step(yh * 4 + lax.rem(x + 2, NX))
    lax.fori_loop(0, 4, lambda i, _: proj_step((1 - yh) * 4 + i), 0)
    PJT[c] = ACC[...].T.astype(BF)
    pj_copy = rcopy(PJT.at[c], PJT.at[c], pj_sem.at[0], pj_sem.at[1], sib)
    pj_copy.start()
    pjx_copy = rcopy(PJT.at[c], PJX.at[c], snd.at[9], pj_sem.at[2], dev(x, y, zq, c))
    pjx_copy.start()
    pltpu.make_async_copy(OG.at[c], OG.at[c], loc_sem.at[1]).wait()
    og_ex.wait()

    def part(j, r):
        def product(t, cls, yl_):
            lhs = (PJT if t < 2 else PJX)[r, :, (t % 2) * 256:(t % 2) * 256 + 256]
            if t >= 2:
                rhs = OGX[t - 2, cls, yl_, j - 2]
            elif j < 2:
                rhs = OG[t, cls, yl_, chunk(j)]
            else:
                rhs = OG[t, cls, yl_, chunk(j), :, pl.ds(pl.multiple_of(p * 128, 128), 128)]
            return jnp.dot(lhs, rhs, preferred_element_type=F32)

        def part_step(i, _):
            cls, yl_ = i // 2, lax.rem(i, 2)
            v = product(0, cls, yl_) + product(1, cls, yl_)
            if j >= 2:
                v = v + product(2, cls, yl_) + product(3, cls, yl_)
            PF[cls, j, yl_, r, :, :, 0:width(j)] = v.reshape(4, 64, width(j))
            PT[cls, j, yl_, r, :, :, 0:width(j)] = v.astype(BF).reshape(4, 64, width(j))
            return 0

        lax.fori_loop(0, 4, part_step, 0, unroll=True)

    def width(j):
        return CW if j < 2 else 128

    KD = (1, 3)

    def half(ref, cls, j, k, h):
        if cls == 0:
            q = yp(k)
            return ref.at[0, j, lax.rem(q, 2), q // 2, 2 * h:2 * h + 2, :, 0:width(j)]
        return ref.at[1, j, h, :, xp(k), :, 0:width(j)]

    relays = {}

    def send_partials(j):
        for cls in range(2):
            for d in range(2):
                cp = rcopy(half(PT, cls, j, 2, d), RL.at[cls, j, d, :, :, 0:width(j)], snd.at[3],
                           r1.at[cls, j, d], line(cls, KD[d]))
                cp.start()
                relays[cls, j, d] = cp
        for cls in range(2):
            for d in range(2):
                rcopy(half(PT, cls, j, KD[d], 1 - d), R1.at[j, cls, d, 1 - d, :, :, 0:width(j)], snd.at[3],
                      rf.at[j], line(cls, KD[d])).start()

    def relay_partials(j):
        w = width(j)
        for d in range(2):
            for cls in range(2):
                relays[cls, j, d].wait_recv()
                both = half(PF, cls, j, KD[d], d)[...] + RL[cls, j, d, :, :, 0:w].astype(F32)
                AGB[cls, j, d, :, :, 0:w] = both.astype(BF)
                rcopy(AGB.at[cls, j, d, :, :, 0:w], R1.at[j, cls, d, d, :, :, 0:w], snd.at[4], rf.at[j],
                      line(cls, KD[d])).start()

    def first_sums(j):
        w = width(j)
        arrived(w // 8, 8192, rf.at[j])

        def total(cls, h):
            v = half(PF, cls, j, 0, h)[...]
            for d in range(2):
                v = v + R1[j, cls, d, h, :, :, 0:w].astype(F32)
            return v

        for h in range(2):
            SB[j, 2 * h:2 * h + 2, :, 0:w] = total(0, h)
            SC[j, h, :, :, 0:w] = total(1, h)
        for k in (2, 1, 3):
            q = yp(k)
            rcopy(SB.at[j, xp(k), :, 0:w], R2.at[j, 0, k - 1, :, 0:w], snd.at[5], r2.at[j],
                  dev(xp(k), y, z, c)).start()
            rcopy(SC.at[j, lax.rem(q, 2), q // 2, :, 0:w], R2.at[j, 1, k - 1, :, 0:w], snd.at[5], r2.at[j],
                  dev(x, q, z, c)).start()

    def second_sums(j):
        w = width(j)
        arrived(48, w * 16, r2.at[j])
        vb = SB[j, x, :, 0:w]
        vc = SC[j, yl, yh, :, 0:w]
        for k in range(3):
            vb = vb + R2[j, 0, k, :, 0:w]
            vc = vc + R2[j, 1, k, :, 0:w]
        if j == NCH - 1:
            R3[5, 0] = vb
            R3[5, 1] = vc
            return
        for i in range(w // 128):
            slot = 2 * j + i
            T3[slot, 0] = vb[:, i * 128:(i + 1) * 128]
            T3[slot, 1] = vc[:, i * 128:(i + 1) * 128]
            to = chunk(j) * ZC + (i if j < 2 else p)
            rcopy(T3.at[slot], R3.at[2 * j + (p if j < 2 else 0)], snd.at[6], rcv.at[2], dev(x, y, to, c)).start()

    for step in range(NCH + 3):
        if step < NCH:
            if step == 2:
                pjx_copy.wait_recv()
                pjx_on = rcopy(PJX.at[c], PJX.at[c], snd.at[9], pj_sem.at[3], sib)
                pjx_on.start()
                arrived(64, 8192, rcv.at[0])
            part(step, c)
            if step == 0:
                pj_copy.wait()
            if step == 2:
                pjx_on.wait_recv()
            part(step, 1 - c)
            send_partials(step)
        if step in (1, 2, 3):
            relay_partials(step - 1)
        if step in (2, 3, 4, 5):
            first_sums(step - 2)
        if step == 3:
            relay_partials(3)
        if step in (3, 4, 5, 6):
            second_sums(step - 3)

    arrived(80, 2048, rcv.at[2])
    g0 = R3[0]
    for k in range(1, 6):
        g0 = g0 + R3[k]
    g = jnp.concatenate([g0[0], g0[1]], axis=1)
    for cp in m_own:
        cp.wait()
    first = beta_one * M1[...] + (1.0 - beta_one) * g
    second = beta_two * M2[...] + (1.0 - beta_two) * g * g
    o1_ref[...] = first
    o2_ref[...] = second
    D[dp] = (first / (jnp.sqrt(second) + adam_epsilon)).astype(BF)
    for dx, dy in ((2, 1), (1, 1), (3, 1), (2, 0), (0, 1), (1, 0), (3, 0)):
        q = lax.rem(yh + dy, 2) * 4 + xp(dx)
        rcopy(D.at[dp], D.at[dp], snd.at[7], rcv.at[3], (q, sh)).start()
    arrived(240, 512, snd.at[0])
    arrived(192, 8192, snd.at[1])
    arrived(48, 8192, snd.at[2])
    arrived(96, 8192, snd.at[3])
    arrived(48, 8192, snd.at[4])
    arrived(144, 4096, snd.at[5])
    arrived(80, 2048, snd.at[6])
    arrived(64, 8192, snd.at[8])
    arrived(32, 8192, snd.at[9])
    lr_copy.wait()
    arrived(112, 1024, rcv.at[3])
    arrived(112, 1024, snd.at[7])
    d_own = D[pl.ds(c * 4, 4)].reshape(256, 256)
    d_sib = D[pl.ds((1 - c) * 4, 4)].reshape(256, 256)
    for b in range(4):
        own = jnp.concatenate([W[h, yh, x, 2 * b:2 * b + 2].reshape(256, 128) for h in range(2)], axis=1)
        oth = jnp.concatenate([LR[h, 2 * b:2 * b + 2].reshape(256, 128) for h in range(2)], axis=1)
        u = jnp.dot(own, d_own, preferred_element_type=F32) + jnp.dot(oth, d_sib, preferred_element_type=F32)
        up_ref[b * 256:(b + 1) * 256, :] = u.astype(BF)


def store_outputs(a_ref, b_ref, u_ref, ao_ref, bo_ref, uo_ref, sem):
    copies = [
        pltpu.make_async_copy(u_ref, uo_ref, sem.at[0]),
        pltpu.make_async_copy(a_ref, ao_ref, sem.at[1]),
        pltpu.make_async_copy(b_ref, bo_ref, sem.at[2]),
    ]
    for cp in copies:
        cp.start()
    for cp in copies:
        cp.wait()


def on_device(tokens, out_grad, projector, first_moment, second_moment):
    vm = pl.BlockSpec(memory_space=pltpu.VMEM)
    hbm = pl.BlockSpec(memory_space=pl.ANY)
    dma = pltpu.SemaphoreType.DMA
    held = pl.pallas_call(
        kernel,
        out_shape=(pltpu.VMEM((64, 256), F32), pltpu.VMEM((64, 256), F32), pltpu.VMEM((1024, 256), BF)),
        in_specs=[pl.BlockSpec(memory_space=pltpu.HBM)] * 5,
        out_specs=(vm, vm, vm),
        scratch_shapes=[
            pltpu.VMEM((2, 256, 8192), BF),
            pltpu.VMEM((2, 2, 2, NCH, 256, CW), BF),
            pltpu.VMEM((2, 2, 2, 2, 256, 128), BF),
            pltpu.VMEM((2, 256, 512), BF),
            pltpu.VMEM((32, 512), BF),
            pltpu.VMEM((64, 256), F32),
            pltpu.VMEM((64, 256), F32),
            pltpu.VMEM((2, 2, 32, 128), BF),
            pltpu.VMEM((2, 2, 4, 8, 2, 64, 128), BF),
            pltpu.VMEM((2, 8, 2, 64, 128), BF),
            pltpu.VMEM((512, 256), F32),
            pltpu.VMEM((2, 256, 512), BF),
            pltpu.VMEM((2, NCH, 2, 2, 4, 64, CW), BF),
            pltpu.VMEM((2, NCH, 2, 2, 4, 64, CW), F32),
            pltpu.VMEM((2, NCH, 2, 2, 64, CW), BF),
            pltpu.VMEM((2, NCH, 2, 2, 64, CW), BF),
            pltpu.VMEM((NCH, 2, 2, 2, 2, 64, CW), BF),
            pltpu.VMEM((NCH, 4, 64, CW), F32),
            pltpu.VMEM((NCH, 2, 2, 64, CW), F32),
            pltpu.VMEM((NCH, 2, 3, 64, CW), F32),
            pltpu.VMEM((5, 2, 64, 128), F32),
            pltpu.VMEM((6, 2, 64, 128), F32),
            pltpu.VMEM((8, 64, 256), BF),
            dma((5,)), dma((2,)), dma((2,)),
            dma((8,)), dma((2, 4)), dma((2, 4, 3)),
            dma((2,)), dma((4,)),
            dma((2, NCH, 2)), dma((NCH,)), dma((NCH,)),
            dma((10,)), dma((4,)),
        ],
        compiler_params=pltpu.CompilerParams(
            collective_id=0, has_side_effects=True, vmem_limit_bytes=56 * 2**20
        ),
        name="galore",
    )(tokens, out_grad, projector, first_moment, second_moment)
    return pl.pallas_call(
        store_outputs,
        out_shape=(
            jax.ShapeDtypeStruct((64, 256), F32),
            jax.ShapeDtypeStruct((64, 256), F32),
            jax.ShapeDtypeStruct((1024, 256), BF),
        ),
        in_specs=[vm, vm, vm],
        out_specs=(hbm, hbm, hbm),
        scratch_shapes=[dma((3,))],
        name="store_outputs",
    )(*[pltpu.with_memory_space_constraint(a, pltpu.VMEM) for a in held])


def solution(mesh):
    in_specs = (
        P(("dp", "shard"), None),
        P(("dp", "shard"), None),
        P(("dp", "shard"), None),
        P("dp", "shard"),
        P("dp", "shard"),
    )
    out_specs = (P("dp", "shard"), P("dp", "shard"), P("dp", "shard"))
    return jax.shard_map(
        on_device, mesh=mesh, in_specs=in_specs, out_specs=out_specs, check_vma=False
    )
```

```python
import jax
import jax.numpy as jnp
from jax import lax
from jax.experimental import pallas as pl
from jax.experimental.pallas import tpu as pltpu
from jax.sharding import PartitionSpec as P

MESH = pl.DeviceIdType.MESH
beta_one = 0.9
beta_two = 0.999
adam_epsilon = 1e-08
NX, NY, NZ = 4, 4, 8
NCH = 4
ZC = NZ // NCH
CW = ZC * 128
BF = jnp.bfloat16
F32 = jnp.float32


def kernel(tok_ref, grad_ref, proj_ref, m1_ref, m2_ref, o1_ref, o2_ref, up_ref,
           T, OG, OGX, PJX, PJ, M1, M2, S, W, LR, U, ACC, PJT, PT, PF, RL, AGB, R1, SB, SC, R2, T3, R3, D,
           loc_sem, ex_s, ex_r, zr, mr, fr, lr_sem, pj_sem, r1, rf, r2, snd, rcv):
    dp = lax.axis_index("dp")
    sh = lax.axis_index("shard")
    x, yh = lax.rem(dp, NX), dp // NX
    z, yl, c = sh // 4, lax.rem(sh // 2, 2), lax.rem(sh, 2)
    y = yh * 2 + yl

    def dev(x_, y_, z_, c_):
        return ((y_ // 2) * NX + x_, z_ * 4 + lax.rem(y_, 2) * 2 + c_)

    def xp(k):
        return lax.rem(x + k, NX)

    def yp(k):
        return lax.rem(y + k, NY)

    def zp(k):
        return lax.rem(z + k, NZ)

    sib = dev(x, y, z, 1 - c)
    p = lax.rem(z, 2)
    zq = z + 1 - 2 * p

    def chunk(j):
        return lax.rem(z // ZC + (1, 3, 2, 0)[j], NCH)

    def arrived(rows, columns, sem):
        ref = T.at[0, 0:rows, 0:columns]
        pltpu.make_async_copy(ref, ref, sem).wait()

    def rcopy(src, dst, ss, rs, device):
        return pltpu.make_async_remote_copy(src_ref=src, dst_ref=dst, send_sem=ss, recv_sem=rs,
                                            device_id=device, device_id_type=MESH)

    barrier = pltpu.get_barrier_semaphore()
    peers = [sib]
    for k in range(1, NZ):
        peers += [dev(x, y, zp(k), c), dev(x, y, zp(k), 1 - c)]
    for k in range(1, 4):
        peers += [dev(xp(k), y, z, c), dev(x, yp(k), z, c), dev(xp(k), yp(2), z, c)]
    for peer in peers:
        pl.semaphore_signal(barrier, inc=1, device_id=peer, device_id_type=MESH)

    tok_own = pltpu.make_async_copy(tok_ref, T.at[c], loc_sem.at[0])
    pj_own = pltpu.make_async_copy(proj_ref, PJ, loc_sem.at[2])
    pj_own.start()
    m_own = [pltpu.make_async_copy(m1_ref, M1, loc_sem.at[3]), pltpu.make_async_copy(m2_ref, M2, loc_sem.at[4])]
    for cp in m_own:
        cp.start()
    tok_own.start()

    def og_src(par, cls, yl_, z_):
        return grad_ref.at[:, pl.ds(pl.multiple_of(z_ * 1024 + yl_ * 512 + par * 256 + cls * 128, 128), 128)]

    def og_dst(cls, yl_, z_):
        return OG.at[c, cls, yl_, z_ // ZC, :, pl.ds((z_ % ZC) * 128, 128)]

    for cls in range(2):
        for yl_ in range(2):
            for z_ in range(NZ):
                pltpu.make_async_copy(og_src(c, cls, yl_, z_), og_dst(cls, yl_, z_), loc_sem.at[1]).start()

    pj_own.wait()
    for h in range(2):
        for cls in range(2):
            S[h, cls] = PJ[:, h * 256 + cls * 128:h * 256 + cls * 128 + 128]
    pl.semaphore_wait(barrier, len(peers))

    W[:, yh, x, z, yl, pl.ds(pl.multiple_of(c * 32, 32), 32), :] = S[c]
    z_order = (0, 1, 7, 2, 6, 3, 5, 4)
    for k in z_order:
        for rel in range(2):
            if k == 0 and rel == 0:
                continue
            t = c if rel == 0 else 1 - c
            cp = rcopy(S.at[t], W.at[:, yh, x, z, yl, pl.ds(pl.multiple_of(c * 32, 32), 32)],
                       snd.at[0], zr.at[k], dev(x, y, zp(k), t))
            cp.start()


    def proj_step(k):
        w0 = W[0, k // 4, lax.rem(k, 4)].reshape(1024, 128)
        w1 = W[1, k // 4, lax.rem(k, 4)].reshape(1024, 128)
        w = jnp.concatenate([w0, w1], axis=1)
        tk = T[:, :, pl.ds(pl.multiple_of(k * 1024, 1024), 1024)].reshape(512, 1024)
        ACC[...] += jnp.dot(tk, w, preferred_element_type=F32)
        return 0


    def line(cls, k):
        return dev(x, yp(k), z, c) if cls == 0 else dev(xp(k), y, z, c)

    def block(cls, j, k, zs_):
        xb = lax.rem(x + NX - (j if cls == 0 else k), NX)
        yb = lax.rem(y + NY - (k if cls == 0 else j), NY)
        return W.at[cls, yb // 2, xb, zs_, lax.rem(yb, 2)]

    whole_z, low_z, high_z = pl.ds(0, NZ), pl.ds(0, NZ // 2), pl.ds(NZ // 2, NZ // 2)

    def send(cls, j, key, blk, k):
        rcopy(blk, blk, snd.at[1], fr.at[cls, j, key], line(cls, k)).start()

    def forward(cls, j):
        for k in (1, 3):
            send(cls, j, k // 2, block(cls, j, 0, whole_z), k)

    def relay(cls, j):
        arrived(16, 4096, fr.at[cls, j, 0])
        send(cls, j, 2, block(cls, j, 1, low_z), 1)
        arrived(16, 4096, fr.at[cls, j, 1])
        send(cls, j, 2, block(cls, j, 3, high_z), 3)

    for k in z_order:
        arrived(16, 512 if k == 0 else 1024, zr.at[k])
        for cls in range(2):
            blk = W.at[cls, yh, x, lax.rem(z + NZ - k, NZ), yl]
            for m in (1, 3, 2):
                to = dev(xp(m), y, z, c) if cls == 0 else dev(x, yp(m), z, c)
                rcopy(blk, blk, snd.at[2], mr.at[cls, m], to).start()
            for m in (1, 3):
                send(cls, 0, m // 2, blk, m)

    tok_ex = rcopy(tok_ref, T.at[c], ex_s.at[0], ex_r.at[0], sib)
    tok_ex.start()
    for cls in range(2):
        for yl_ in range(2):
            for z_ in range(NZ):
                rcopy(og_src(1 - c, cls, yl_, z_), og_dst(cls, yl_, z_), ex_s.at[1], ex_r.at[1], sib).start()
    og_ex = rcopy(OG.at[c], OG.at[1 - c], ex_s.at[1], ex_r.at[1], sib)
    for jj in range(2):
        for cls in range(2):
            for yl_ in range(2):
                for c_ in range(2):
                    rcopy(og_src(c_, cls, yl_, chunk(2 + jj) * ZC + 1 - p), OGX.at[c, cls, yl_, jj],
                          snd.at[8], rcv.at[0], dev(x, y, zq, c_)).start()

    for j in (1, 3, 2):
        for cls in range(2):
            arrived(16, 4096, mr.at[cls, j])
            forward(cls, j)
        for cls in range(2):
            relay(cls, 0 if j == 1 else 1 if j == 3 else 3)
    for cls in range(2):
        relay(cls, 2)
    tok_own.wait()
    tok_ex.wait()
    ACC[...] = jnp.zeros_like(ACC)
    for j in (0, 1, 3):
        for cls in range(2):
            arrived(16, 4096, fr.at[cls, j, 2])
    lax.fori_loop(0, 3, lambda i, _: proj_step(yh * 4 + lax.rem(x + 3 + i, NX)), 0)
    for cls in range(2):
        arrived(16, 4096, fr.at[cls, 2, 2])

    lr_copy = rcopy(W.at[:, yh, x], LR.at[c], lr_sem.at[0], lr_sem.at[1], sib)
    lr_copy.start()
    lr_own = pltpu.make_async_copy(W.at[:, yh, x], LR.at[c], loc_sem.at[5])
    lr_own.start()
    proj_step(yh * 4 + lax.rem(x + 2, NX))
    lax.fori_loop(0, 4, lambda i, _: proj_step((1 - yh) * 4 + i), 0)
    PJT[c] = ACC[...].T.astype(BF)
    pj_copy = rcopy(PJT.at[c], PJT.at[c], pj_sem.at[0], pj_sem.at[1], sib)
    pj_copy.start()
    pjx_copy = rcopy(PJT.at[c], PJX.at[c], snd.at[9], pj_sem.at[2], dev(x, y, zq, c))
    pjx_copy.start()
    pltpu.make_async_copy(OG.at[c], OG.at[c], loc_sem.at[1]).wait()
    og_ex.wait()

    def part(j, r):
        def product(t, cls, yl_):
            lhs = (PJT if t < 2 else PJX)[r, :, (t % 2) * 256:(t % 2) * 256 + 256]
            if t >= 2:
                rhs = OGX[t - 2, cls, yl_, j - 2]
            elif j < 2:
                rhs = OG[t, cls, yl_, chunk(j)]
            else:
                rhs = OG[t, cls, yl_, chunk(j), :, pl.ds(pl.multiple_of(p * 128, 128), 128)]
            return jnp.dot(lhs, rhs, preferred_element_type=F32)

        def part_step(i, _):
            cls, yl_ = i // 2, lax.rem(i, 2)
            v = product(0, cls, yl_) + product(1, cls, yl_)
            if j >= 2:
                v = v + product(2, cls, yl_) + product(3, cls, yl_)
            PF[cls, j, yl_, r, :, :, 0:width(j)] = v.reshape(4, 64, width(j))
            PT[cls, j, yl_, r, :, :, 0:width(j)] = v.astype(BF).reshape(4, 64, width(j))
            return 0

        lax.fori_loop(0, 4, part_step, 0, unroll=True)

    def width(j):
        return CW if j < 2 else 128

    KD = (1, 3)

    def half(ref, cls, j, k, h):
        if cls == 0:
            q = yp(k)
            return ref.at[0, j, lax.rem(q, 2), q // 2, 2 * h:2 * h + 2, :, 0:width(j)]
        return ref.at[1, j, h, :, xp(k), :, 0:width(j)]

    relays = {}

    def send_partials(j):
        for cls in range(2):
            for d in range(2):
                cp = rcopy(half(PT, cls, j, 2, d), RL.at[cls, j, d, :, :, 0:width(j)], snd.at[3],
                           r1.at[cls, j, d], line(cls, KD[d]))
                cp.start()
                relays[cls, j, d] = cp
        for cls in range(2):
            for d in range(2):
                rcopy(half(PT, cls, j, KD[d], 1 - d), R1.at[j, cls, d, 1 - d, :, :, 0:width(j)], snd.at[3],
                      rf.at[j], line(cls, KD[d])).start()

    def relay_partials(j):
        w = width(j)
        for d in range(2):
            for cls in range(2):
                relays[cls, j, d].wait_recv()
                both = half(PF, cls, j, KD[d], d)[...] + RL[cls, j, d, :, :, 0:w].astype(F32)
                AGB[cls, j, d, :, :, 0:w] = both.astype(BF)
                rcopy(AGB.at[cls, j, d, :, :, 0:w], R1.at[j, cls, d, d, :, :, 0:w], snd.at[4], rf.at[j],
                      line(cls, KD[d])).start()

    def first_sums(j):
        w = width(j)
        arrived(w // 8, 8192, rf.at[j])

        def total(cls, h):
            v = half(PF, cls, j, 0, h)[...]
            for d in range(2):
                v = v + R1[j, cls, d, h, :, :, 0:w].astype(F32)
            return v

        for h in range(2):
            SB[j, 2 * h:2 * h + 2, :, 0:w] = total(0, h)
            SC[j, h, :, :, 0:w] = total(1, h)
        for k in (2, 1, 3):
            q = yp(k)
            rcopy(SB.at[j, xp(k), :, 0:w], R2.at[j, 0, k - 1, :, 0:w], snd.at[5], r2.at[j],
                  dev(xp(k), y, z, c)).start()
            rcopy(SC.at[j, lax.rem(q, 2), q // 2, :, 0:w], R2.at[j, 1, k - 1, :, 0:w], snd.at[5], r2.at[j],
                  dev(x, q, z, c)).start()

    def second_sums(j):
        w = width(j)
        arrived(48, w * 16, r2.at[j])
        vb = SB[j, x, :, 0:w]
        vc = SC[j, yl, yh, :, 0:w]
        for k in range(3):
            vb = vb + R2[j, 0, k, :, 0:w]
            vc = vc + R2[j, 1, k, :, 0:w]
        if j == NCH - 1:
            R3[5, 0] = vb
            R3[5, 1] = vc
            return
        for i in range(w // 128):
            slot = 2 * j + i
            T3[slot, 0] = vb[:, i * 128:(i + 1) * 128]
            T3[slot, 1] = vc[:, i * 128:(i + 1) * 128]
            to = chunk(j) * ZC + (i if j < 2 else p)
            rcopy(T3.at[slot], R3.at[2 * j + (p if j < 2 else 0)], snd.at[6], rcv.at[2], dev(x, y, to, c)).start()

    def partials(j):
        if j == 2:
            pjx_copy.wait_recv()
            pjx_on = rcopy(PJX.at[c], PJX.at[c], snd.at[9], pj_sem.at[3], sib)
            pjx_on.start()
            arrived(64, 8192, rcv.at[0])
        part(j, c)
        if j == 0:
            pj_copy.wait()
        if j == 2:
            pjx_on.wait_recv()
        part(j, 1 - c)
        send_partials(j)

    partials(0)
    partials(1)
    relay_partials(0)
    partials(2)
    relay_partials(1)
    first_sums(0)
    partials(3)
    relay_partials(2)
    first_sums(1)
    second_sums(0)
    relay_partials(3)
    first_sums(2)
    second_sums(1)
    first_sums(3)
    second_sums(2)
    second_sums(3)

    arrived(80, 2048, rcv.at[2])
    g0 = R3[0]
    for k in range(1, 6):
        g0 = g0 + R3[k]
    g = jnp.concatenate([g0[0], g0[1]], axis=1)
    for cp in m_own:
        cp.wait()
    first = beta_one * M1[...] + (1.0 - beta_one) * g
    second = beta_two * M2[...] + (1.0 - beta_two) * g * g
    o1_ref[...] = first
    o2_ref[...] = second
    D[dp] = (first / (jnp.sqrt(second) + adam_epsilon)).astype(BF)
    for dx, dy in ((2, 1), (1, 1), (3, 1), (2, 0), (0, 1), (1, 0), (3, 0)):
        q = lax.rem(yh + dy, 2) * 4 + xp(dx)
        rcopy(D.at[dp], D.at[dp], snd.at[7], rcv.at[3 if dy == 0 else 1], (q, sh)).start()
    arrived(240, 512, snd.at[0])
    arrived(192, 8192, snd.at[1])
    arrived(48, 8192, snd.at[2])
    arrived(96, 8192, snd.at[3])
    arrived(48, 8192, snd.at[4])
    arrived(144, 4096, snd.at[5])
    arrived(80, 2048, snd.at[6])
    arrived(64, 8192, snd.at[8])
    arrived(32, 8192, snd.at[9])
    lr_copy.wait()
    lr_own.wait()

    def rows(h, b):
        return jnp.concatenate([LR[h, cls, 2 * b:2 * b + 2].reshape(256, 128) for cls in range(2)], axis=1)

    arrived(48, 1024, rcv.at[3])
    near = D[pl.ds(yh * 4, 4)].reshape(256, 256)
    for b in range(4):
        U[b * 256:(b + 1) * 256, :] = jnp.dot(rows(yh, b), near, preferred_element_type=F32)
    arrived(112, 1024, snd.at[7])
    arrived(64, 1024, rcv.at[1])
    far = D[pl.ds((1 - yh) * 4, 4)].reshape(256, 256)
    for b in range(4):
        u = U[b * 256:(b + 1) * 256, :] + jnp.dot(rows(1 - yh, b), far, preferred_element_type=F32)
        up_ref[b * 256:(b + 1) * 256, :] = u.astype(BF)


def store_outputs(a_ref, b_ref, u_ref, ao_ref, bo_ref, uo_ref, sem):
    copies = [
        pltpu.make_async_copy(u_ref, uo_ref, sem.at[0]),
        pltpu.make_async_copy(a_ref, ao_ref, sem.at[1]),
        pltpu.make_async_copy(b_ref, bo_ref, sem.at[2]),
    ]
    for cp in copies:
        cp.start()
    for cp in copies:
        cp.wait()


def on_device(tokens, out_grad, projector, first_moment, second_moment):
    vm = pl.BlockSpec(memory_space=pltpu.VMEM)
    hbm = pl.BlockSpec(memory_space=pl.ANY)
    dma = pltpu.SemaphoreType.DMA
    held = pl.pallas_call(
        kernel,
        out_shape=(pltpu.VMEM((64, 256), F32), pltpu.VMEM((64, 256), F32), pltpu.VMEM((1024, 256), BF)),
        in_specs=[pl.BlockSpec(memory_space=pltpu.HBM)] * 5,
        out_specs=(vm, vm, vm),
        scratch_shapes=[
            pltpu.VMEM((2, 256, 8192), BF),
            pltpu.VMEM((2, 2, 2, NCH, 256, CW), BF),
            pltpu.VMEM((2, 2, 2, 2, 256, 128), BF),
            pltpu.VMEM((2, 256, 512), BF),
            pltpu.VMEM((32, 512), BF),
            pltpu.VMEM((64, 256), F32),
            pltpu.VMEM((64, 256), F32),
            pltpu.VMEM((2, 2, 32, 128), BF),
            pltpu.VMEM((2, 2, 4, 8, 2, 64, 128), BF),
            pltpu.VMEM((2, 2, 8, 2, 64, 128), BF),
            pltpu.VMEM((1024, 256), F32),
            pltpu.VMEM((512, 256), F32),
            pltpu.VMEM((2, 256, 512), BF),
            pltpu.VMEM((2, NCH, 2, 2, 4, 64, CW), BF),
            pltpu.VMEM((2, NCH, 2, 2, 4, 64, CW), F32),
            pltpu.VMEM((2, NCH, 2, 2, 64, CW), BF),
            pltpu.VMEM((2, NCH, 2, 2, 64, CW), BF),
            pltpu.VMEM((NCH, 2, 2, 2, 2, 64, CW), BF),
            pltpu.VMEM((NCH, 4, 64, CW), F32),
            pltpu.VMEM((NCH, 2, 2, 64, CW), F32),
            pltpu.VMEM((NCH, 2, 3, 64, CW), F32),
            pltpu.VMEM((5, 2, 64, 128), F32),
            pltpu.VMEM((6, 2, 64, 128), F32),
            pltpu.VMEM((8, 64, 256), BF),
            dma((6,)), dma((2,)), dma((2,)),
            dma((8,)), dma((2, 4)), dma((2, 4, 3)),
            dma((2,)), dma((4,)),
            dma((2, NCH, 2)), dma((NCH,)), dma((NCH,)),
            dma((10,)), dma((4,)),
        ],
        compiler_params=pltpu.CompilerParams(
            collective_id=0, has_side_effects=True, vmem_limit_bytes=56 * 2**20
        ),
        name="galore",
    )(tokens, out_grad, projector, first_moment, second_moment)
    return pl.pallas_call(
        store_outputs,
        out_shape=(
            jax.ShapeDtypeStruct((64, 256), F32),
            jax.ShapeDtypeStruct((64, 256), F32),
            jax.ShapeDtypeStruct((1024, 256), BF),
        ),
        in_specs=[vm, vm, vm],
        out_specs=(hbm, hbm, hbm),
        scratch_shapes=[dma((3,))],
        name="store_outputs",
    )(*[pltpu.with_memory_space_constraint(a, pltpu.VMEM) for a in held])


def solution(mesh):
    in_specs = (
        P(("dp", "shard"), None),
        P(("dp", "shard"), None),
        P(("dp", "shard"), None),
        P("dp", "shard"),
        P("dp", "shard"),
    )
    out_specs = (P("dp", "shard"), P("dp", "shard"), P("dp", "shard"))
    return jax.shard_map(
        on_device, mesh=mesh, in_specs=in_specs, out_specs=out_specs, check_vma=False
    )
```

```python
import jax
import jax.numpy as jnp
from jax import lax
from jax.experimental import pallas as pl
from jax.experimental.pallas import tpu as pltpu
from jax.sharding import PartitionSpec as P

MESH = pl.DeviceIdType.MESH
beta_one = 0.9
beta_two = 0.999
adam_epsilon = 1e-08
NX, NY, NZ = 4, 4, 8
NCH = 4
ZC = NZ // NCH
CW = ZC * 128
BF = jnp.bfloat16
F32 = jnp.float32


def kernel(tok_ref, grad_ref, proj_ref, m1_ref, m2_ref, o1_ref, o2_ref, up_ref,
           T, OG, OGX, PJX, PJ, M1, M2, S, W, LR, U, ACC, PJT, PT, PF, RL, AGB, R1, SB, SC, R2, T3, R3, D,
           loc_sem, ex_s, ex_r, zr, mr, fr, lr_sem, pj_sem, r1, rf, r2, snd, rcv):
    dp = lax.axis_index("dp")
    sh = lax.axis_index("shard")
    x, yh = lax.rem(dp, NX), dp // NX
    z, yl, c = sh // 4, lax.rem(sh // 2, 2), lax.rem(sh, 2)
    y = yh * 2 + yl

    def dev(x_, y_, z_, c_):
        return ((y_ // 2) * NX + x_, z_ * 4 + lax.rem(y_, 2) * 2 + c_)

    def xp(k):
        return lax.rem(x + k, NX)

    def yp(k):
        return lax.rem(y + k, NY)

    def zp(k):
        return lax.rem(z + k, NZ)

    sib = dev(x, y, z, 1 - c)
    p = lax.rem(z, 2)
    zq = z + 1 - 2 * p

    def chunk(j):
        return lax.rem(z // ZC + (1, 3, 2, 0)[j], NCH)

    def arrived(rows, columns, sem):
        ref = T.at[0, 0:rows, 0:columns]
        pltpu.make_async_copy(ref, ref, sem).wait()

    def rcopy(src, dst, ss, rs, device):
        return pltpu.make_async_remote_copy(src_ref=src, dst_ref=dst, send_sem=ss, recv_sem=rs,
                                            device_id=device, device_id_type=MESH)

    barrier = pltpu.get_barrier_semaphore()
    peers = [sib]
    for k in range(1, NZ):
        peers += [dev(x, y, zp(k), c), dev(x, y, zp(k), 1 - c)]
    for k in range(1, 4):
        peers += [dev(xp(k), y, z, c), dev(x, yp(k), z, c), dev(xp(k), yp(2), z, c)]
    for peer in peers:
        pl.semaphore_signal(barrier, inc=1, device_id=peer, device_id_type=MESH)

    tok_own = pltpu.make_async_copy(tok_ref, T.at[c], loc_sem.at[0])
    pj_own = pltpu.make_async_copy(proj_ref, PJ, loc_sem.at[2])
    pj_own.start()
    m_own = [pltpu.make_async_copy(m1_ref, M1, loc_sem.at[3]), pltpu.make_async_copy(m2_ref, M2, loc_sem.at[4])]
    for cp in m_own:
        cp.start()
    tok_own.start()

    def og_src(par, cls, yl_, z_):
        return grad_ref.at[:, pl.ds(pl.multiple_of(z_ * 1024 + yl_ * 512 + par * 256 + cls * 128, 128), 128)]

    def og_dst(cls, yl_, z_):
        return OG.at[c, cls, yl_, z_ // ZC, :, pl.ds((z_ % ZC) * 128, 128)]

    for cls in range(2):
        for yl_ in range(2):
            for z_ in range(NZ):
                pltpu.make_async_copy(og_src(c, cls, yl_, z_), og_dst(cls, yl_, z_), loc_sem.at[1]).start()

    pj_own.wait()
    for h in range(2):
        for cls in range(2):
            S[h, cls] = PJ[:, h * 256 + cls * 128:h * 256 + cls * 128 + 128]
    pl.semaphore_wait(barrier, len(peers))

    W[:, yh, x, z, yl, pl.ds(pl.multiple_of(c * 32, 32), 32), :] = S[c]
    z_order = (0, 1, 7, 2, 6, 3, 5, 4)
    for k in z_order:
        for rel in range(2):
            if k == 0 and rel == 0:
                continue
            t = c if rel == 0 else 1 - c
            cp = rcopy(S.at[t], W.at[:, yh, x, z, yl, pl.ds(pl.multiple_of(c * 32, 32), 32)],
                       snd.at[0], zr.at[k], dev(x, y, zp(k), t))
            cp.start()


    def proj_step(k):
        w0 = W[0, k // 4, lax.rem(k, 4)].reshape(1024, 128)
        w1 = W[1, k // 4, lax.rem(k, 4)].reshape(1024, 128)
        w = jnp.concatenate([w0, w1], axis=1)
        tk = T[:, :, pl.ds(pl.multiple_of(k * 1024, 1024), 1024)].reshape(512, 1024)
        ACC[...] += jnp.dot(tk, w, preferred_element_type=F32)
        return 0


    def line(cls, k):
        return dev(x, yp(k), z, c) if cls == 0 else dev(xp(k), y, z, c)

    def block(cls, j, k, zs_):
        xb = lax.rem(x + NX - (j if cls == 0 else k), NX)
        yb = lax.rem(y + NY - (k if cls == 0 else j), NY)
        return W.at[cls, yb // 2, xb, zs_, lax.rem(yb, 2)]

    whole_z, low_z, high_z = pl.ds(0, NZ), pl.ds(0, NZ // 2), pl.ds(NZ // 2, NZ // 2)

    def send(cls, j, key, blk, k):
        rcopy(blk, blk, snd.at[1], fr.at[cls, j, key], line(cls, k)).start()

    def forward(cls, j):
        for k in (1, 3):
            send(cls, j, k // 2, block(cls, j, 0, whole_z), k)

    def relay(cls, j):
        arrived(16, 4096, fr.at[cls, j, 0])
        send(cls, j, 2, block(cls, j, 1, low_z), 1)
        arrived(16, 4096, fr.at[cls, j, 1])
        send(cls, j, 2, block(cls, j, 3, high_z), 3)

    for k in z_order:
        arrived(16, 512 if k == 0 else 1024, zr.at[k])
        for cls in range(2):
            blk = W.at[cls, yh, x, lax.rem(z + NZ - k, NZ), yl]
            for m in (1, 3, 2):
                to = dev(xp(m), y, z, c) if cls == 0 else dev(x, yp(m), z, c)
                rcopy(blk, blk, snd.at[2], mr.at[cls, m], to).start()
            for m in (1, 3):
                send(cls, 0, m // 2, blk, m)

    tok_ex = rcopy(tok_ref, T.at[c], ex_s.at[0], ex_r.at[0], sib)
    tok_ex.start()
    for cls in range(2):
        for yl_ in range(2):
            for z_ in range(NZ):
                rcopy(og_src(1 - c, cls, yl_, z_), og_dst(cls, yl_, z_), ex_s.at[1], ex_r.at[1], sib).start()
    og_ex = rcopy(OG.at[c], OG.at[1 - c], ex_s.at[1], ex_r.at[1], sib)
    for jj in range(2):
        for cls in range(2):
            for yl_ in range(2):
                for c_ in range(2):
                    rcopy(og_src(c_, cls, yl_, chunk(2 + jj) * ZC + 1 - p), OGX.at[c, cls, yl_, jj],
                          snd.at[8], rcv.at[0], dev(x, y, zq, c_)).start()

    for j in (1, 3, 2):
        for cls in range(2):
            arrived(16, 4096, mr.at[cls, j])
            forward(cls, j)
    for j in (0, 1, 3, 2):
        for cls in range(2):
            relay(cls, j)
    tok_own.wait()
    tok_ex.wait()
    ACC[...] = jnp.zeros_like(ACC)
    for j in (0, 1, 3):
        for cls in range(2):
            arrived(16, 4096, fr.at[cls, j, 2])
    lax.fori_loop(0, 3, lambda i, _: proj_step(yh * 4 + lax.rem(x + 3 + i, NX)), 0)
    for cls in range(2):
        arrived(16, 4096, fr.at[cls, 2, 2])

    lr_copy = rcopy(W.at[:, yh, x], LR.at[c], lr_sem.at[0], lr_sem.at[1], sib)
    lr_copy.start()
    lr_own = pltpu.make_async_copy(W.at[:, yh, x], LR.at[c], loc_sem.at[5])
    lr_own.start()
    proj_step(yh * 4 + lax.rem(x + 2, NX))
    lax.fori_loop(0, 4, lambda i, _: proj_step((1 - yh) * 4 + i), 0)
    PJT[c] = ACC[...].T.astype(BF)
    pj_copy = rcopy(PJT.at[c], PJT.at[c], pj_sem.at[0], pj_sem.at[1], sib)
    pj_copy.start()
    pjx_copy = rcopy(PJT.at[c], PJX.at[c], snd.at[9], pj_sem.at[2], dev(x, y, zq, c))
    pjx_copy.start()
    pltpu.make_async_copy(OG.at[c], OG.at[c], loc_sem.at[1]).wait()
    og_ex.wait()

    def part(j, r):
        def product(t, cls, yl_):
            lhs = (PJT if t < 2 else PJX)[r, :, (t % 2) * 256:(t % 2) * 256 + 256]
            if t >= 2:
                rhs = OGX[t - 2, cls, yl_, j - 2]
            elif j < 2:
                rhs = OG[t, cls, yl_, chunk(j)]
            else:
                rhs = OG[t, cls, yl_, chunk(j), :, pl.ds(pl.multiple_of(p * 128, 128), 128)]
            return jnp.dot(lhs, rhs, preferred_element_type=F32)

        def part_step(i, _):
            cls, yl_ = i // 2, lax.rem(i, 2)
            v = product(0, cls, yl_) + product(1, cls, yl_)
            if j >= 2:
                v = v + product(2, cls, yl_) + product(3, cls, yl_)
            PF[cls, j, yl_, r, :, :, 0:width(j)] = v.reshape(4, 64, width(j))
            PT[cls, j, yl_, r, :, :, 0:width(j)] = v.astype(BF).reshape(4, 64, width(j))
            return 0

        lax.fori_loop(0, 4, part_step, 0, unroll=True)

    def width(j):
        return CW if j < 2 else 128

    KD = (1, 3)

    def half(ref, cls, j, k, h):
        if cls == 0:
            q = yp(k)
            return ref.at[0, j, lax.rem(q, 2), q // 2, 2 * h:2 * h + 2, :, 0:width(j)]
        return ref.at[1, j, h, :, xp(k), :, 0:width(j)]

    relays = {}

    def send_partials(j):
        for cls in range(2):
            for d in range(2):
                cp = rcopy(half(PT, cls, j, 2, d), RL.at[cls, j, d, :, :, 0:width(j)], snd.at[3],
                           r1.at[cls, j, d], line(cls, KD[d]))
                cp.start()
                relays[cls, j, d] = cp
        for cls in range(2):
            for d in range(2):
                rcopy(half(PT, cls, j, KD[d], 1 - d), R1.at[j, cls, d, 1 - d, :, :, 0:width(j)], snd.at[3],
                      rf.at[j], line(cls, KD[d])).start()

    def relay_partials(j):
        w = width(j)
        for d in range(2):
            for cls in range(2):
                relays[cls, j, d].wait_recv()
                both = half(PF, cls, j, KD[d], d)[...] + RL[cls, j, d, :, :, 0:w].astype(F32)
                AGB[cls, j, d, :, :, 0:w] = both.astype(BF)
                rcopy(AGB.at[cls, j, d, :, :, 0:w], R1.at[j, cls, d, d, :, :, 0:w], snd.at[4], rf.at[j],
                      line(cls, KD[d])).start()

    def first_sums(j):
        w = width(j)
        arrived(w // 8, 8192, rf.at[j])

        def total(cls, h):
            v = half(PF, cls, j, 0, h)[...]
            for d in range(2):
                v = v + R1[j, cls, d, h, :, :, 0:w].astype(F32)
            return v

        for h in range(2):
            SB[j, 2 * h:2 * h + 2, :, 0:w] = total(0, h)
            SC[j, h, :, :, 0:w] = total(1, h)
        for k in (2, 1, 3):
            q = yp(k)
            rcopy(SB.at[j, xp(k), :, 0:w], R2.at[j, 0, k - 1, :, 0:w], snd.at[5], r2.at[j],
                  dev(xp(k), y, z, c)).start()
            rcopy(SC.at[j, lax.rem(q, 2), q // 2, :, 0:w], R2.at[j, 1, k - 1, :, 0:w], snd.at[5], r2.at[j],
                  dev(x, q, z, c)).start()

    def second_sums(j):
        w = width(j)
        arrived(48, w * 16, r2.at[j])
        vb = SB[j, x, :, 0:w]
        vc = SC[j, yl, yh, :, 0:w]
        for k in range(3):
            vb = vb + R2[j, 0, k, :, 0:w]
            vc = vc + R2[j, 1, k, :, 0:w]
        if j == NCH - 1:
            R3[5, 0] = vb
            R3[5, 1] = vc
            return
        for i in range(w // 128):
            slot = 2 * j + i
            T3[slot, 0] = vb[:, i * 128:(i + 1) * 128]
            T3[slot, 1] = vc[:, i * 128:(i + 1) * 128]
            to = chunk(j) * ZC + (i if j < 2 else p)
            rcopy(T3.at[slot], R3.at[2 * j + (p if j < 2 else 0)], snd.at[6], rcv.at[2], dev(x, y, to, c)).start()

    def partials(j):
        if j == 2:
            pjx_copy.wait_recv()
            pjx_on = rcopy(PJX.at[c], PJX.at[c], snd.at[9], pj_sem.at[3], sib)
            pjx_on.start()
            arrived(64, 8192, rcv.at[0])
        part(j, c)
        if j == 0:
            pj_copy.wait()
        if j == 2:
            pjx_on.wait_recv()
        part(j, 1 - c)
        send_partials(j)

    partials(0)
    partials(1)
    relay_partials(0)
    partials(2)
    relay_partials(1)
    first_sums(0)
    partials(3)
    relay_partials(2)
    first_sums(1)
    second_sums(0)
    relay_partials(3)
    first_sums(2)
    second_sums(1)
    first_sums(3)
    second_sums(2)
    second_sums(3)

    arrived(80, 2048, rcv.at[2])
    g0 = R3[0]
    for k in range(1, 6):
        g0 = g0 + R3[k]
    g = jnp.concatenate([g0[0], g0[1]], axis=1)
    for cp in m_own:
        cp.wait()
    first = beta_one * M1[...] + (1.0 - beta_one) * g
    second = beta_two * M2[...] + (1.0 - beta_two) * g * g
    o1_ref[...] = first
    o2_ref[...] = second
    D[dp] = (first / (jnp.sqrt(second) + adam_epsilon)).astype(BF)
    for dx, dy in ((2, 1), (1, 1), (3, 1), (2, 0), (0, 1), (1, 0), (3, 0)):
        q = lax.rem(yh + dy, 2) * 4 + xp(dx)
        rcopy(D.at[dp], D.at[dp], snd.at[7], rcv.at[3 if dy == 0 else 1], (q, sh)).start()
    arrived(240, 512, snd.at[0])
    arrived(192, 8192, snd.at[1])
    arrived(48, 8192, snd.at[2])
    arrived(96, 8192, snd.at[3])
    arrived(48, 8192, snd.at[4])
    arrived(144, 4096, snd.at[5])
    arrived(80, 2048, snd.at[6])
    arrived(64, 8192, snd.at[8])
    arrived(32, 8192, snd.at[9])
    lr_copy.wait()
    lr_own.wait()

    def rows(h, b):
        return jnp.concatenate([LR[h, cls, 2 * b:2 * b + 2].reshape(256, 128) for cls in range(2)], axis=1)

    arrived(48, 1024, rcv.at[3])
    near = D[pl.ds(yh * 4, 4)].reshape(256, 256)
    for b in range(4):
        U[b * 256:(b + 1) * 256, :] = jnp.dot(rows(yh, b), near, preferred_element_type=F32)
    arrived(112, 1024, snd.at[7])
    arrived(64, 1024, rcv.at[1])
    far = D[pl.ds((1 - yh) * 4, 4)].reshape(256, 256)
    for b in range(4):
        u = U[b * 256:(b + 1) * 256, :] + jnp.dot(rows(1 - yh, b), far, preferred_element_type=F32)
        up_ref[b * 256:(b + 1) * 256, :] = u.astype(BF)


def store_outputs(a_ref, b_ref, u_ref, ao_ref, bo_ref, uo_ref, sem):
    copies = [
        pltpu.make_async_copy(u_ref, uo_ref, sem.at[0]),
        pltpu.make_async_copy(a_ref, ao_ref, sem.at[1]),
        pltpu.make_async_copy(b_ref, bo_ref, sem.at[2]),
    ]
    for cp in copies:
        cp.start()
    for cp in copies:
        cp.wait()


def on_device(tokens, out_grad, projector, first_moment, second_moment):
    vm = pl.BlockSpec(memory_space=pltpu.VMEM)
    hbm = pl.BlockSpec(memory_space=pl.ANY)
    dma = pltpu.SemaphoreType.DMA
    held = pl.pallas_call(
        kernel,
        out_shape=(pltpu.VMEM((64, 256), F32), pltpu.VMEM((64, 256), F32), pltpu.VMEM((1024, 256), BF)),
        in_specs=[pl.BlockSpec(memory_space=pltpu.HBM)] * 5,
        out_specs=(vm, vm, vm),
        scratch_shapes=[
            pltpu.VMEM((2, 256, 8192), BF),
            pltpu.VMEM((2, 2, 2, NCH, 256, CW), BF),
            pltpu.VMEM((2, 2, 2, 2, 256, 128), BF),
            pltpu.VMEM((2, 256, 512), BF),
            pltpu.VMEM((32, 512), BF),
            pltpu.VMEM((64, 256), F32),
            pltpu.VMEM((64, 256), F32),
            pltpu.VMEM((2, 2, 32, 128), BF),
            pltpu.VMEM((2, 2, 4, 8, 2, 64, 128), BF),
            pltpu.VMEM((2, 2, 8, 2, 64, 128), BF),
            pltpu.VMEM((1024, 256), F32),
            pltpu.VMEM((512, 256), F32),
            pltpu.VMEM((2, 256, 512), BF),
            pltpu.VMEM((2, NCH, 2, 2, 4, 64, CW), BF),
            pltpu.VMEM((2, NCH, 2, 2, 4, 64, CW), F32),
            pltpu.VMEM((2, NCH, 2, 2, 64, CW), BF),
            pltpu.VMEM((2, NCH, 2, 2, 64, CW), BF),
            pltpu.VMEM((NCH, 2, 2, 2, 2, 64, CW), BF),
            pltpu.VMEM((NCH, 4, 64, CW), F32),
            pltpu.VMEM((NCH, 2, 2, 64, CW), F32),
            pltpu.VMEM((NCH, 2, 3, 64, CW), F32),
            pltpu.VMEM((5, 2, 64, 128), F32),
            pltpu.VMEM((6, 2, 64, 128), F32),
            pltpu.VMEM((8, 64, 256), BF),
            dma((6,)), dma((2,)), dma((2,)),
            dma((8,)), dma((2, 4)), dma((2, 4, 3)),
            dma((2,)), dma((4,)),
            dma((2, NCH, 2)), dma((NCH,)), dma((NCH,)),
            dma((10,)), dma((4,)),
        ],
        compiler_params=pltpu.CompilerParams(
            collective_id=0, has_side_effects=True, vmem_limit_bytes=56 * 2**20
        ),
        name="galore",
    )(tokens, out_grad, projector, first_moment, second_moment)
    return pl.pallas_call(
        store_outputs,
        out_shape=(
            jax.ShapeDtypeStruct((64, 256), F32),
            jax.ShapeDtypeStruct((64, 256), F32),
            jax.ShapeDtypeStruct((1024, 256), BF),
        ),
        in_specs=[vm, vm, vm],
        out_specs=(hbm, hbm, hbm),
        scratch_shapes=[dma((3,))],
        name="store_outputs",
    )(*[pltpu.with_memory_space_constraint(a, pltpu.VMEM) for a in held])


def solution(mesh):
    in_specs = (
        P(("dp", "shard"), None),
        P(("dp", "shard"), None),
        P(("dp", "shard"), None),
        P("dp", "shard"),
        P("dp", "shard"),
    )
    out_specs = (P("dp", "shard"), P("dp", "shard"), P("dp", "shard"))
    return jax.shard_map(
        on_device, mesh=mesh, in_specs=in_specs, out_specs=out_specs, check_vma=False
    )
```
